32 devices in a mesh: dp: 16 (over z, y, x), mp: 2 (over core).
Axes of the slice: x: 2, y: 2, z: 4, core: 2. Of those that a mesh axis runs over, the one named last changes fastest.
Arguments:
- train_in: bfloat16 [1024, 64, 16], P('dp'), may hold values from -6 to 6
- train_out_grad: bfloat16 [1024, 64, 1024], P('dp', None, 'mp'), may hold values from -6 to 6
- query_in: bfloat16 [1024, 64, 16], P('dp'), may hold values from -6 to 6
- query_out_grad: bfloat16 [1024, 64, 1024], P('dp', None, 'mp'), may hold values from -6 to 6
- query_owner: int32 [1024, 1], P('dp'), may hold values from 0 to 15; in each aligned block of 64 rows (0 to 63, 64 to 127, ...) at most 8 rows name the same one
- sketch_seed: int32 [1], replicated, may hold values from 0 to 1073741823
Outputs:
- kernel: float32 [1024, 1024], P('mp', 'dp')
- owner_scores: float32 [16, 16, 8, 64], P('dp')
The draws below stay inside these ranges and needn't reach their ends.
Inputs may be any that keep to these rules, and one draw needn't show every extreme that they name: `query_owner`: within the queries of one device (aligned blocks of 64), one owner is named at most 8 times, a bound that some block reaches in every draw.
All inputs are finite; a program needn't handle non-finite values.
Results may differ from the reference program's by a relative error of at most 0.0041.
Values may be sent and summed in bfloat16 or wider, within the bound.
A program may use at most 64 MiB of HBM per device.

```python
import math
import jax
import jax.numpy as jnp
import numpy as np
from jax import lax

VW = 1024
R = 16
K = 8192
L = 64
EX_DEV = 64
QX_DEV = 64
TRAIN_ROWS = 1024
QUERY_ROWS = 1024
CAP = 8
N_DP = 16


def block_levels(rng, extent, pieces, smallest, largest):
    def one(position, parts):
        draws = jax.random.uniform(jax.random.fold_in(jax.random.fold_in(rng, 6), position), (parts,), jnp.float32, smallest / len(pieces), largest / len(pieces))
        return jnp.repeat(jnp.exp(draws), extent[position] // parts).reshape((-1,) + (1,) * (len(extent) - position - 1))

    loudness = one(*pieces[0])
    for cut in pieces[1:]:
        loudness = loudness * one(*cut)
    return loudness


def routed_block(stream_key, own, number, rows, amount, top, limit, lean):
    ranking = jax.random.permutation(stream_key, amount)
    crowded, common = shares(amount, rows * top, limit, lean, True), shares(amount, rows * top, limit, lean, False)
    places = jnp.arange(amount)

    def named(sizes, turn):
        used = int((sizes > 0).sum())
        fixed = max(1, used // 4)
        shifted = fixed + (places - fixed + turn * (used - fixed)) % max(1, amount - fixed)
        return jnp.zeros((amount,), jnp.int32).at[ranking[jnp.where(places < fixed, places, shifted)]].set(jnp.asarray(sizes, jnp.int32))

    sizes = jnp.where(number % 4 == 0, named(crowded, number // 4), named(common, number - number // 4 - 1))
    mixed = jax.random.permutation(jax.random.fold_in(own, 3), amount)
    giver, taker = mixed[0:amount // 2 * 2:2], mixed[1:amount // 2 * 2:2]
    margin = jnp.minimum(sizes[giver] - 1, limit - sizes[taker]) // 2
    margin = jnp.where((giver == ranking[0]) | (taker == ranking[0]) | (sizes[taker] == 0), 0, jnp.maximum(margin, 0))
    shifted = jax.random.randint(jax.random.fold_in(own, 4), (amount // 2,), 0, 1 << 20) % (margin + 1)
    sizes = sizes.at[giver].add(-shifted).at[taker].add(shifted)
    items = jnp.searchsorted(jnp.cumsum(sizes), jnp.arange(rows * top), side="right").astype(jnp.int32)
    listing = items.reshape(top, rows).T
    listing = listing[jax.random.permutation(jax.random.fold_in(own, 1), rows)]
    turn = jax.random.randint(jax.random.fold_in(own, 2), (rows, 1), 0, top)
    return jnp.take_along_axis(listing, (jnp.arange(top)[None, :] + turn) % top, axis=1)


def shares(number_of, total, bound, lean, full):
    portions = [(1 << 20) // math.isqrt(grade ** lean) + 1 for grade in range(1, number_of + 1)]
    largest = bound if full else min(bound, max(-(-total // number_of), total * portions[0] // sum(portions)))
    least = 1 if total - largest >= number_of - 1 else 0
    holding, rest = [largest] + [least] * (number_of - 1), total - largest - least * (number_of - 1)
    while rest > 0:
        free = [i for i in range(1, number_of) if holding[i] < largest] or [i for i in range(1, number_of) if holding[i] < bound]
        mass, remaining = sum([portions[i] for i in free]), rest
        for i in free:
            extra = min(bound - holding[i], max(1, remaining * portions[i] // mass), rest)
            holding[i] = holding[i] + extra
            rest = rest - extra
    return np.array(holding)


def centred(rng, shape, spread, most, split=(), kind=jnp.bfloat16):
    loudness = block_levels(rng, shape, split, -0.22, 0.18) if split else 1.0
    array = jax.random.normal(rng, shape, jnp.float32) * spread * loudness
    return jnp.minimum(jnp.maximum(array, -most), most).astype(kind)


def setup_inputs(seed: int = 0) -> dict:
    keys = jax.random.split(jax.random.key(seed), 7)
    train_in = centred(keys[0], (TRAIN_ROWS, L, R), 1.0, 6.0, ((0, 16),))
    train_out_grad = centred(keys[1], (TRAIN_ROWS, L, VW), 1.0, 6.0, ((0, 16), (2, 2)))
    query_in = centred(keys[2], (QUERY_ROWS, L, R), 1.0, 6.0, ((0, 16),))
    query_out_grad = centred(keys[3], (QUERY_ROWS, L, VW), 1.0, 6.0, ((0, 16), (2, 2)))
    query_owner_keys = jax.random.split(jax.random.fold_in(keys[4], 1), QUERY_ROWS // QX_DEV)
    query_owner_turns = jax.random.permutation(jax.random.fold_in(keys[4], 3), QUERY_ROWS // QX_DEV)
    query_owner = jax.vmap(lambda own, number: routed_block(jax.random.fold_in(keys[4], 2), own, number, QX_DEV, N_DP, 1, CAP, 2))(query_owner_keys, query_owner_turns).reshape((QUERY_ROWS, 1))
    sketch_seed = jax.random.randint(keys[5], (1,), 0, 1073741824).astype(jnp.int32)
    return {"train_in": train_in, "train_out_grad": train_out_grad, "query_in": query_in, "query_out_grad": query_out_grad, "query_owner": query_owner, "sketch_seed": sketch_seed}


hash_factor = 73244475

def sign_table(coords, columns, seed_word):
    mixing = coords[:, None] * K + columns[None, :] ^ seed_word
    for round_index in range(2):
        mixing = mixing * hash_factor
        mixing = mixing ^ lax.shift_right_logical(mixing, jnp.full_like(mixing, 16))
    return (1 - 2 * (mixing & 1)).astype(jnp.bfloat16)

def local_grads(packed):
    inputs, out_grads = packed
    return jnp.einsum('ntr,ntj->nrj', inputs.astype(jnp.float32), out_grads.astype(jnp.float32)).astype(jnp.bfloat16)

def reference(train_in, train_out_grad, query_in, query_out_grad, query_owner, sketch_seed):
    seed_word = sketch_seed[0]
    train_grads = lax.map(local_grads, (train_in.reshape(N_DP, EX_DEV, L, R), train_out_grad.reshape(N_DP, EX_DEV, L, VW)))
    train_grads = train_grads.reshape(TRAIN_ROWS, R * VW)
    query_grads = lax.map(local_grads, (query_in.reshape(N_DP, QX_DEV, L, R), query_out_grad.reshape(N_DP, QX_DEV, L, VW)))
    query_grads = query_grads.reshape(N_DP, QX_DEV, R * VW)
    coords = lax.iota(jnp.int32, R * VW)
    step_cols = min(1024, K)

    def project_block(offset):
        columns = offset + lax.iota(jnp.int32, step_cols)
        return jnp.dot(train_grads, sign_table(coords, columns, seed_word), preferred_element_type=jnp.float32)
    col_blocks = lax.map(project_block, jnp.arange(0, K, step_cols, dtype=jnp.int32))
    feature_scale = 1.0 / math.sqrt(L * R * VW)
    features = (jnp.transpose(col_blocks, (1, 0, 2)).reshape(TRAIN_ROWS, K) * feature_scale).astype(jnp.bfloat16)
    kernel = jnp.dot(features, features.T, preferred_element_type=jnp.float32) * (1.0 / math.sqrt(K))
    owners = query_owner[:, 0].reshape(N_DP, QX_DEV)
    later_index = lax.broadcasted_iota(jnp.int32, (QX_DEV, QX_DEV), 0)
    earlier = lax.broadcasted_iota(jnp.int32, (QX_DEV, QX_DEV), 1) < later_index
    same_owner = owners[:, :, None] == owners[:, None, :]
    slot_rank = lax.optimization_barrier(jnp.sum((same_owner & earlier[None]).astype(jnp.int32), axis=2))
    train_by_owner = train_grads.reshape(N_DP, EX_DEV, R * VW)

    def score_device(packed):
        grads_here, owners_here = packed
        chosen = train_by_owner[owners_here]
        return jnp.einsum('qc,qnc->qn', grads_here.astype(jnp.float32), chosen.astype(jnp.float32), precision=lax.Precision.HIGHEST)
    scores = lax.map(score_device, (query_grads, owners))
    score_scale = 1.0 / (L * math.sqrt(R * VW))
    sources = lax.broadcasted_iota(jnp.int32, (N_DP, QX_DEV), 0)
    owner_scores = jnp.zeros((N_DP, N_DP, CAP, EX_DEV), jnp.float32)
    owner_scores = owner_scores.at[owners, sources, slot_rank].set(scores * score_scale)
    return (kernel, owner_scores)
```

```python
import math

import jax
import jax.numpy as jnp
from jax import lax
from jax.sharding import PartitionSpec as P

VW = 1024
R = 16
K = 8192
L = 64
PIECES = 4

hash_factor = 73244475


def as_word(value):
    value &= 0xFFFFFFFF
    return value - (1 << 32) if value >= 1 << 31 else value


last_factor = as_word((hash_factor + 65536) << 15)


def sign_table(coords, columns, seed_word):
    high = ((coords * K) ^ (seed_word & ~(K - 1))) * hash_factor
    low = (columns ^ (seed_word & (K - 1))) * hash_factor
    mixing = high[:, None] + low[None, :]
    mixing = mixing ^ lax.shift_right_logical(mixing, jnp.full_like(mixing, 16))
    mixing = mixing * last_factor
    return jnp.where(mixing < 0, jnp.float32(-1), jnp.float32(1)).astype(jnp.bfloat16)


def local_grads(inputs, out_grads):
    return jnp.einsum("ntr,ntj->nrj", inputs, out_grads, preferred_element_type=jnp.float32).astype(
        jnp.bfloat16
    )


def shards(train_in, train_out_grad, query_in, query_out_grad, query_owner, sketch_seed):
    seed_word = sketch_seed[0]
    mp_index = lax.axis_index("mp")
    dp_index = lax.axis_index("dp")
    n_mp = lax.axis_size("mp")
    n_dp = lax.axis_size("dp")
    group = 2 if n_dp % 2 == 0 else 1
    local_width = train_out_grad.shape[2]
    examples = train_in.shape[0]

    with jax.named_scope("queries"):
        query_grads = local_grads(query_in, query_out_grad)
        queries = query_grads.shape[0]
        capacity = 2 * queries // n_dp
        owners = query_owner[:, 0]
        later_index = lax.broadcasted_iota(jnp.int32, (queries, queries), 0)
        earlier = (owners[:, None] == owners[None, :]) & (
            lax.broadcasted_iota(jnp.int32, (queries, queries), 1) < later_index
        )
        slot_rank = jnp.sum(earlier.astype(jnp.int32), axis=1)
        target = owners * capacity + slot_rank
        placing = (
            lax.broadcasted_iota(jnp.int32, (n_dp * capacity, queries), 0) == target[None, :]
        ).astype(jnp.bfloat16)
        flat_queries = query_grads.reshape(queries, R * local_width)
        outgoing = jnp.dot(placing, flat_queries, preferred_element_type=jnp.float32).astype(
            jnp.bfloat16
        )
        outgoing = outgoing.reshape(n_dp, capacity, R * local_width)

    with jax.named_scope("train"):
        train_grads = local_grads(train_in, train_out_grad)
        flat_train = train_grads.reshape(examples, R * local_width)

    with jax.named_scope("project"):
        feature_scale = 1.0 / math.sqrt(L * R * VW)
        n_cols = K // (group * n_mp)
        place = dp_index % group
        columns = (place * n_mp + mp_index) * n_cols + lax.iota(jnp.int32, n_cols)
        ranks = R // PIECES
        swap = [(d, d ^ 1) for d in range(n_dp)]
        total = None
        for piece in range(PIECES):
            own = flat_train[:, piece * ranks * local_width : (piece + 1) * ranks * local_width]
            if group == 2:
                other = lax.ppermute(own, "dp", swap)
                both = jnp.where(
                    place == 0,
                    jnp.concatenate([own, other], axis=0),
                    jnp.concatenate([other, own], axis=0),
                )
            else:
                both = own
            for step in range(n_mp):
                held = both
                if step:
                    held = lax.ppermute(
                        both, "mp", [(m, (m - step) % n_mp) for m in range(n_mp)]
                    )
                part = (mp_index + step) % n_mp
                rank_ids = piece * ranks + lax.broadcasted_iota(
                    jnp.int32, (ranks, local_width), 0
                )
                unit_ids = lax.broadcasted_iota(jnp.int32, (ranks, local_width), 1)
                coords = (rank_ids * VW + part * local_width + unit_ids).reshape(-1)
                term = jnp.dot(
                    held,
                    sign_table(coords, columns, seed_word),
                    preferred_element_type=jnp.float32,
                )
                total = term if total is None else total + term
        features = (total * feature_scale).astype(jnp.bfloat16)

    with jax.named_scope("gram"):
        sharing = [[d for d in range(n_dp) if d % group == g] for g in range(group)]
        blocks = lax.all_to_all(
            features, "dp", split_axis=1, concat_axis=0, tiled=True, axis_index_groups=sharing
        )
        wide = [blocks]
        for step in range(1, n_mp):
            wide.append(
                lax.ppermute(blocks, "mp", [(m, (m - step) % n_mp) for m in range(n_mp)])
            )
        wide = jnp.concatenate(wide, axis=1)
        n_rows = wide.shape[0] // n_mp
        rows = lax.dynamic_slice_in_dim(wide, mp_index * n_rows, n_rows, axis=0)
        partial = lax.dot_general(
            wide, rows, (((1,), (1,)), ((), ())), preferred_element_type=jnp.float32
        ).astype(jnp.bfloat16)
        partial = lax.all_to_all(
            partial.reshape(n_dp, examples, n_rows), "dp", split_axis=0, concat_axis=0, tiled=True
        )
        gram = jnp.sum(partial.astype(jnp.float32), axis=0) * (1.0 / math.sqrt(K))

    with jax.named_scope("scores"):
        scores = jnp.einsum(
            "sic,nc->sin",
            lax.all_to_all(outgoing, "dp", split_axis=0, concat_axis=0, tiled=True),
            flat_train,
            preferred_element_type=jnp.float32,
        )
        score_scale = 1.0 / (L * math.sqrt(R * VW))
        scores = lax.psum(scores, "mp") * score_scale
    return (gram.T, scores[None])


def solution(mesh):
    return jax.shard_map(
        shards,
        mesh=mesh,
        in_specs=(
            P("dp", None, None),
            P("dp", None, "mp"),
            P("dp", None, None),
            P("dp", None, "mp"),
            P("dp", None),
            P(),
        ),
        out_specs=(P("mp", "dp"), P("dp", None, None, None)),
        check_vma=False,
    )
```

```python
import math

import jax
import jax.numpy as jnp
from jax import lax
from jax.sharding import PartitionSpec as P

VW = 1024
R = 16
K = 8192
L = 64
PIECES = 4

hash_factor = 73244475


def as_word(value):
    value &= 0xFFFFFFFF
    return value - (1 << 32) if value >= 1 << 31 else value


last_factor = as_word((hash_factor + 65536) << 15)


def sign_table(coords, columns, seed_word):
    high = ((coords * K) ^ (seed_word & ~(K - 1))) * hash_factor
    low = (columns ^ (seed_word & (K - 1))) * hash_factor
    mixing = high[:, None] + low[None, :]
    mixing = mixing ^ lax.shift_right_logical(mixing, jnp.full_like(mixing, 16))
    mixing = mixing * last_factor
    return jnp.where(mixing < 0, jnp.float32(-1), jnp.float32(1)).astype(jnp.bfloat16)


def local_grads(inputs, out_grads):
    return jnp.einsum("ntr,ntj->nrj", inputs, out_grads, preferred_element_type=jnp.float32).astype(
        jnp.bfloat16
    )


def shards(train_in, train_out_grad, query_in, query_out_grad, query_owner, sketch_seed):
    seed_word = sketch_seed[0]
    mp_index = lax.axis_index("mp")
    dp_index = lax.axis_index("dp")
    n_mp = lax.axis_size("mp")
    n_dp = lax.axis_size("dp")
    group = 2 if n_dp % 2 == 0 else 1
    local_width = train_out_grad.shape[2]
    examples = train_in.shape[0]

    with jax.named_scope("queries"):
        query_grads = local_grads(query_in, query_out_grad)
        queries = query_grads.shape[0]
        capacity = 2 * queries // n_dp
        owners = query_owner[:, 0]
        later_index = lax.broadcasted_iota(jnp.int32, (queries, queries), 0)
        earlier = (owners[:, None] == owners[None, :]) & (
            lax.broadcasted_iota(jnp.int32, (queries, queries), 1) < later_index
        )
        slot_rank = jnp.sum(earlier.astype(jnp.int32), axis=1)
        target = owners * capacity + slot_rank
        placing = (
            lax.broadcasted_iota(jnp.int32, (n_dp * capacity, queries), 0) == target[None, :]
        ).astype(jnp.bfloat16)
        flat_queries = query_grads.reshape(queries, R * local_width)
        outgoing = jnp.dot(placing, flat_queries, preferred_element_type=jnp.float32).astype(
            jnp.bfloat16
        )
        outgoing = outgoing.reshape(n_dp, capacity, R * local_width)

        routed = lax.all_to_all(outgoing, "dp", split_axis=0, concat_axis=0, tiled=True)

    with jax.named_scope("train"):
        train_grads = local_grads(train_in, train_out_grad)
        flat_train = train_grads.reshape(examples, R * local_width)

    with jax.named_scope("project"):
        feature_scale = 1.0 / math.sqrt(L * R * VW)
        n_cols = K // (group * n_mp)
        place = dp_index % group
        columns = (place * n_mp + mp_index) * n_cols + lax.iota(jnp.int32, n_cols)
        ranks = R // PIECES
        swap = [(d, d ^ 1) for d in range(n_dp)]
        total = None
        for piece in range(PIECES):
            own = flat_train[:, piece * ranks * local_width : (piece + 1) * ranks * local_width]
            if group == 2:
                other = lax.ppermute(own, "dp", swap)
                both = jnp.where(
                    place == 0,
                    jnp.concatenate([own, other], axis=0),
                    jnp.concatenate([other, own], axis=0),
                )
            else:
                both = own
            for step in range(n_mp):
                held = both
                if step:
                    held = lax.ppermute(
                        both, "mp", [(m, (m - step) % n_mp) for m in range(n_mp)]
                    )
                part = (mp_index + step) % n_mp
                rank_ids = piece * ranks + lax.broadcasted_iota(
                    jnp.int32, (ranks, local_width), 0
                )
                unit_ids = lax.broadcasted_iota(jnp.int32, (ranks, local_width), 1)
                coords = (rank_ids * VW + part * local_width + unit_ids).reshape(-1)
                term = jnp.dot(
                    held,
                    sign_table(coords, columns, seed_word),
                    preferred_element_type=jnp.float32,
                )
                total = term if total is None else total + term
        features = (total * feature_scale).astype(jnp.bfloat16)
        features, routed = lax.optimization_barrier((features, routed))

    with jax.named_scope("gram"):
        sharing = [[d for d in range(n_dp) if d % group == g] for g in range(group)]
        blocks = lax.all_to_all(
            features, "dp", split_axis=1, concat_axis=0, tiled=True, axis_index_groups=sharing
        )
        wide = [blocks]
        for step in range(1, n_mp):
            wide.append(
                lax.ppermute(blocks, "mp", [(m, (m - step) % n_mp) for m in range(n_mp)])
            )
        wide = jnp.concatenate(wide, axis=1)
        n_rows = wide.shape[0] // n_mp
        rows = lax.dynamic_slice_in_dim(wide, mp_index * n_rows, n_rows, axis=0)
        partial = lax.dot_general(
            wide, rows, (((1,), (1,)), ((), ())), preferred_element_type=jnp.float32
        ).astype(jnp.bfloat16)
        partial = lax.all_to_all(
            partial.reshape(n_dp, examples, n_rows), "dp", split_axis=0, concat_axis=0, tiled=True
        )
        gram = jnp.sum(partial.astype(jnp.float32), axis=0) * (1.0 / math.sqrt(K))

    with jax.named_scope("scores"):
        scores = jnp.einsum(
            "sic,nc->sin",
            routed,
            flat_train,
            preferred_element_type=jnp.float32,
        )
        score_scale = 1.0 / (L * math.sqrt(R * VW))
        scores = lax.psum(scores, "mp") * score_scale
    return (gram.T, scores[None])


def solution(mesh):
    return jax.shard_map(
        shards,
        mesh=mesh,
        in_specs=(
            P("dp", None, None),
            P("dp", None, "mp"),
            P("dp", None, None),
            P("dp", None, "mp"),
            P("dp", None),
            P(),
        ),
        out_specs=(P("mp", "dp"), P("dp", None, None, None)),
        check_vma=False,
    )
```

```python
import functools
import math

import jax
import jax.numpy as jnp
from jax import lax
from jax.experimental import pallas as pl
from jax.experimental.pallas import tpu as pltpu
from jax.sharding import PartitionSpec as P

VW = 1024
R = 16
K = 8192
L = 64
PIECES = 4

hash_factor = 73244475


def as_word(value):
    value &= 0xFFFFFFFF
    return value - (1 << 32) if value >= 1 << 31 else value


last_factor = as_word((hash_factor + 65536) << 15)


def sign_table(coords, columns, seed_word):
    high = ((coords * K) ^ (seed_word & ~(K - 1))) * hash_factor
    low = (columns ^ (seed_word & (K - 1))) * hash_factor
    mixing = high[:, None] + low[None, :]
    mixing = mixing ^ lax.shift_right_logical(mixing, jnp.full_like(mixing, 16))
    mixing = mixing * last_factor
    return jnp.where(mixing < 0, jnp.float32(-1), jnp.float32(1)).astype(jnp.bfloat16)


def local_grads(inputs, out_grads):
    return jnp.einsum("ntr,ntj->nrj", inputs, out_grads, preferred_element_type=jnp.float32).astype(
        jnp.bfloat16
    )


MESH = pl.DeviceIdType.MESH


def finish_kernel(
    n_mp,
    blocks_ref,
    routed_ref,
    train_ref,
    gram_ref,
    scores_ref,
    wide,
    keep,
    xout,
    xin,
    gout,
    gin,
    parts,
    feat_sems,
    fwd_sems,
    pair_sems,
    gram_sems,
    score_sems,
):
    n_pairs, pair_rows, _ = blocks_ref.shape
    examples = pair_rows // 2
    n_rows = n_pairs * pair_rows // n_mp
    dp = lax.axis_index("dp")
    mp = lax.axis_index("mp")
    pair = dp // 2
    side = dp % 2
    mate = pair * 2 + 1 - side
    others = n_pairs - 1

    def later(i):
        return lax.rem(pair + 1 + i, n_pairs)

    def core(step):
        return lax.rem(mp + step, n_mp)

    def feat_copy(target, source):
        return pltpu.make_async_remote_copy(
            src_ref=blocks_ref.at[target],
            dst_ref=wide.at[mp, source],
            send_sem=feat_sems.at[0, target],
            recv_sem=feat_sems.at[1, source],
            device_id=(target * 2 + side, mp),
            device_id_type=MESH,
        )

    def fwd_copy(step, part, source):
        return pltpu.make_async_remote_copy(
            src_ref=wide.at[part, source],
            dst_ref=wide.at[part, source],
            send_sem=fwd_sems.at[0, step - 1, source],
            recv_sem=fwd_sems.at[1, step - 1, source],
            device_id=(dp, core(step)),
            device_id_type=MESH,
        )

    def pair_copy(target):
        return pltpu.make_async_remote_copy(
            src_ref=xout.at[target],
            dst_ref=xin.at[target],
            send_sem=pair_sems.at[0, target],
            recv_sem=pair_sems.at[1, target],
            device_id=(mate, mp),
            device_id_type=MESH,
        )

    def gram_copy(target, source):
        return pltpu.make_async_remote_copy(
            src_ref=gout.at[target],
            dst_ref=gin.at[source],
            send_sem=gram_sems.at[0, target],
            recv_sem=gram_sems.at[1, source],
            device_id=(target * 2 + side, mp),
            device_id_type=MESH,
        )

    def score_copy(step, part):
        return pltpu.make_async_remote_copy(
            src_ref=parts.at[part],
            dst_ref=parts.at[part],
            send_sem=score_sems.at[0, step - 1],
            recv_sem=score_sems.at[1, step - 1],
            device_id=(dp, core(step)),
            device_id_type=MESH,
        )

    barrier = pltpu.get_barrier_semaphore()

    @pl.loop(0, others)
    def _(i):
        pl.semaphore_signal(
            barrier, inc=1, device_id=(later(i) * 2 + side, mp), device_id_type=MESH
        )

    pl.semaphore_signal(barrier, inc=1, device_id=(mate, mp), device_id_type=MESH)
    for step in range(1, n_mp):
        pl.semaphore_signal(barrier, inc=1, device_id=(dp, core(step)), device_id_type=MESH)
    pl.semaphore_wait(barrier, others + n_mp)

    @pl.loop(0, others)
    def _(i):
        feat_copy(later(i), pair).start()

    wide[mp, pair] = blocks_ref[pair]
    for step in range(1, n_mp):
        fwd_copy(step, mp, pair).start()

    width = train_ref.shape[1]
    chunk = min(width, 1024)
    parts[mp] = jnp.zeros(parts.shape[1:], jnp.float32)

    @pl.loop(0, width // chunk)
    def _(i):
        part = pl.ds(pl.multiple_of(i * chunk, chunk), chunk)
        parts[mp] += lax.dot_general(
            routed_ref[:, part],
            train_ref[:, part],
            (((1,), (1,)), ((), ())),
            preferred_element_type=jnp.float32,
        )

    for step in range(1, n_mp):
        score_copy(step, mp).start()

    @pl.loop(0, others)
    def _(i):
        source = lax.rem(pair + others - i, n_pairs)
        feat_copy(source, source).wait_recv()
        for step in range(1, n_mp):
            fwd_copy(step, mp, source).start()

    @pl.loop(0, n_pairs)
    def _(source):
        for step in range(1, n_mp):
            fwd_copy(step, core(n_mp - step), source).wait_recv()

    row_pairs = n_pairs // n_mp
    row_part = pl.ds(mp * row_pairs, row_pairs)

    @pl.loop(0, n_pairs)
    def _(i):
        target = later(i)
        total = None
        for part in range(n_mp):
            term = lax.dot_general(
                wide[part, target],
                wide[part, row_part].reshape(n_rows, -1),
                (((1,), (1,)), ((), ())),
                preferred_element_type=jnp.float32,
            )
            total = term if total is None else total + term
        keep[target] = total.reshape(2, examples, n_rows)
        xout[target] = keep[target, 1 - side].astype(xout.dtype)
        pair_copy(target).start()

    @pl.loop(0, others)
    def _(i):
        target = later(i)
        pair_copy(target).wait_recv()
        gout[target] = (keep[target, side] + xin[target].astype(jnp.float32)).astype(gout.dtype)
        gram_copy(target, pair).start()

    pair_copy(pair).wait_recv()
    gram_ref[...] = keep[pair, side] + xin[pair].astype(jnp.float32)

    for step in range(1, n_mp):
        score_copy(step, core(n_mp - step)).wait_recv()
    summed = parts[0]
    for part in range(1, n_mp):
        summed = summed + parts[part]
    scores_ref[...] = summed * (1.0 / (L * math.sqrt(R * VW)))

    @pl.loop(0, others)
    def _(i):
        source = lax.rem(pair + others - i, n_pairs)
        gram_copy(source, source).wait_recv()
        gram_ref[...] += gin[source].astype(jnp.float32)

    gram_ref[...] = gram_ref[...] * (1.0 / math.sqrt(K))

    @pl.loop(0, others)
    def _(i):
        feat_copy(later(i), pair).wait_send()
        gram_copy(later(i), pair).wait_send()

    @pl.loop(0, n_pairs)
    def _(source):
        pair_copy(source).wait_send()
        for step in range(1, n_mp):
            fwd_copy(step, mp, source).wait_send()

    for step in range(1, n_mp):
        score_copy(step, mp).wait_send()


def finish(blocks, routed, train, n_mp):
    n_pairs, pair_rows, n_cols = blocks.shape
    examples = pair_rows // 2
    n_rows = n_pairs * pair_rows // n_mp
    tile = (n_pairs, examples, n_rows)
    vmem = pl.BlockSpec(memory_space=pltpu.VMEM)
    return pl.pallas_call(
        functools.partial(finish_kernel, n_mp),
        out_shape=(
            jax.ShapeDtypeStruct((examples, n_rows), jnp.float32),
            jax.ShapeDtypeStruct((routed.shape[0], examples), jnp.float32),
        ),
        in_specs=[vmem] * 3,
        out_specs=(vmem, vmem),
        scratch_shapes=[
            pltpu.VMEM((n_mp,) + blocks.shape, jnp.bfloat16),
            pltpu.VMEM((n_pairs, 2, examples, n_rows), jnp.float32),
            pltpu.VMEM(tile, jnp.bfloat16),
            pltpu.VMEM(tile, jnp.bfloat16),
            pltpu.VMEM(tile, jnp.bfloat16),
            pltpu.VMEM(tile, jnp.bfloat16),
            pltpu.VMEM((n_mp, routed.shape[0], examples), jnp.float32),
            pltpu.SemaphoreType.DMA((2, n_pairs)),
            pltpu.SemaphoreType.DMA((2, n_mp - 1, n_pairs)),
            pltpu.SemaphoreType.DMA((2, n_pairs)),
            pltpu.SemaphoreType.DMA((2, n_pairs)),
            pltpu.SemaphoreType.DMA((2, n_mp - 1)),
        ],
        compiler_params=pltpu.CompilerParams(
            collective_id=0, has_side_effects=True, vmem_limit_bytes=44 * 2**20
        ),
        name="finish",
    )(blocks, routed, train)


def shards(train_in, train_out_grad, query_in, query_out_grad, query_owner, sketch_seed):
    seed_word = sketch_seed[0]
    mp_index = lax.axis_index("mp")
    dp_index = lax.axis_index("dp")
    n_mp = lax.axis_size("mp")
    n_dp = lax.axis_size("dp")
    group = 2 if n_dp % 2 == 0 else 1
    local_width = train_out_grad.shape[2]
    examples = train_in.shape[0]

    with jax.named_scope("queries"):
        query_grads = local_grads(query_in, query_out_grad)
        queries = query_grads.shape[0]
        capacity = 2 * queries // n_dp
        owners = query_owner[:, 0]
        later_index = lax.broadcasted_iota(jnp.int32, (queries, queries), 0)
        earlier = (owners[:, None] == owners[None, :]) & (
            lax.broadcasted_iota(jnp.int32, (queries, queries), 1) < later_index
        )
        slot_rank = jnp.sum(earlier.astype(jnp.int32), axis=1)
        target = owners * capacity + slot_rank
        placing = (
            lax.broadcasted_iota(jnp.int32, (n_dp * capacity, queries), 0) == target[None, :]
        ).astype(jnp.bfloat16)
        flat_queries = query_grads.reshape(queries, R * local_width)
        outgoing = jnp.dot(placing, flat_queries, preferred_element_type=jnp.float32).astype(
            jnp.bfloat16
        )
        outgoing = outgoing.reshape(n_dp, capacity, R * local_width)

        routed = lax.all_to_all(outgoing, "dp", split_axis=0, concat_axis=0, tiled=True)

    with jax.named_scope("train"):
        train_grads = local_grads(train_in, train_out_grad)
        flat_train = train_grads.reshape(examples, R * local_width)

    with jax.named_scope("project"):
        feature_scale = 1.0 / math.sqrt(L * R * VW)
        n_cols = K // (group * n_mp)
        place = dp_index % group
        columns = (place * n_mp + mp_index) * n_cols + lax.iota(jnp.int32, n_cols)
        ranks = R // PIECES
        swap = [(d, d ^ 1) for d in range(n_dp)]
        total = None
        for piece in range(PIECES):
            own = flat_train[:, piece * ranks * local_width : (piece + 1) * ranks * local_width]
            if group == 2:
                other = lax.ppermute(own, "dp", swap)
                both = jnp.where(
                    place == 0,
                    jnp.concatenate([own, other], axis=0),
                    jnp.concatenate([other, own], axis=0),
                )
            else:
                both = own
            for step in range(n_mp):
                held = both
                if step:
                    held = lax.ppermute(
                        both, "mp", [(m, (m - step) % n_mp) for m in range(n_mp)]
                    )
                part = (mp_index + step) % n_mp
                rank_ids = piece * ranks + lax.broadcasted_iota(
                    jnp.int32, (ranks, local_width), 0
                )
                unit_ids = lax.broadcasted_iota(jnp.int32, (ranks, local_width), 1)
                coords = (rank_ids * VW + part * local_width + unit_ids).reshape(-1)
                term = jnp.dot(
                    held,
                    sign_table(coords, columns, seed_word),
                    preferred_element_type=jnp.float32,
                )
                total = term if total is None else total + term
        features = (total * feature_scale).astype(jnp.bfloat16)
        features, routed = lax.optimization_barrier((features, routed))

    with jax.named_scope("gram"):
        n_pairs = n_dp // group
        fblocks = features.reshape(group * examples, n_pairs, n_cols // n_pairs).transpose(1, 0, 2)
        gram, scores = finish(fblocks, routed.reshape(n_dp * capacity, -1), flat_train, n_mp)
        scores = scores.reshape(n_dp, capacity, examples)
    return (gram.T, scores[None])


def solution(mesh):
    return jax.shard_map(
        shards,
        mesh=mesh,
        in_specs=(
            P("dp", None, None),
            P("dp", None, "mp"),
            P("dp", None, None),
            P("dp", None, "mp"),
            P("dp", None),
            P(),
        ),
        out_specs=(P("mp", "dp"), P("dp", None, None, None)),
        check_vma=False,
    )
```

```python
import functools
import math

import jax
import jax.numpy as jnp
from jax import lax
from jax.experimental import pallas as pl
from jax.experimental.pallas import tpu as pltpu
from jax.sharding import PartitionSpec as P

VW = 1024
R = 16
K = 8192
L = 64
BLOCK = 64
ROWS = 16
AHEAD = 2

hash_factor = 73244475


def as_word(value):
    value &= 0xFFFFFFFF
    return value - (1 << 32) if value >= 1 << 31 else value


last_factor = as_word((hash_factor + 65536) << 15)


def local_grads(inputs, out_grads):
    return jnp.einsum("ntr,ntj->rnj", inputs, out_grads, preferred_element_type=jnp.float32).astype(
        jnp.bfloat16
    )


MESH = pl.DeviceIdType.MESH


def trak_kernel(
    n_mp,
    early,
    seed_ref,
    train_ref,
    query_ref,
    placing_ref,
    select_ref,
    gram_ref,
    scores_ref,
    held,
    table,
    acc,
    blocks_ref,
    qout,
    routed_ref,
    wide,
    keep,
    xout,
    xin,
    gout,
    gin,
    parts,
    rank_sems,
    core_sems,
    query_sems,
    feat_sems,
    fwd_sems,
    pair_sems,
    gram_sems,
    score_sems,
):
    n_pairs, pair_rows, cols = blocks_ref.shape
    n_dp = routed_ref.shape[0]
    n_tiles, _, tile_cols = table.shape
    per_tile = tile_cols // cols
    width = train_ref.shape[2]
    n_splits = placing_ref.shape[0]
    split_ranks = R // n_splits
    examples = pair_rows // 2
    n_rows = n_pairs * pair_rows // n_mp
    dp = lax.axis_index("dp")
    mp = lax.axis_index("mp")
    pair = dp // 2
    side = dp % 2
    mate = pair * 2 + 1 - side
    others = n_pairs - 1

    def later(i):
        return lax.rem(pair + 1 + i, n_pairs)

    def core(step):
        return lax.rem(mp + step, n_mp)

    def rank_copy(rank, rows):
        return pltpu.make_async_remote_copy(
            src_ref=train_ref.at[rank],
            dst_ref=held.at[mp, rank, rows],
            send_sem=rank_sems.at[0, rank],
            recv_sem=rank_sems.at[1, rank],
            device_id=(mate, mp),
            device_id_type=MESH,
        )

    def core_copy(step, part, rank):
        return pltpu.make_async_remote_copy(
            src_ref=held.at[part, rank],
            dst_ref=held.at[part, rank],
            send_sem=core_sems.at[0, step - 1, rank],
            recv_sem=core_sems.at[1, step - 1, rank],
            device_id=(dp, core(step)),
            device_id_type=MESH,
        )

    def query_copy(target, source):
        return pltpu.make_async_remote_copy(
            src_ref=qout.at[target],
            dst_ref=routed_ref.at[source],
            send_sem=query_sems.at[0, target],
            recv_sem=query_sems.at[1, source],
            device_id=(target, mp),
            device_id_type=MESH,
        )

    def feat_copy(target, source):
        return pltpu.make_async_remote_copy(
            src_ref=blocks_ref.at[target],
            dst_ref=wide.at[mp, source],
            send_sem=feat_sems.at[0, target],
            recv_sem=feat_sems.at[1, source],
            device_id=(target * 2 + side, mp),
            device_id_type=MESH,
        )

    def fwd_copy(step, part, source):
        return pltpu.make_async_remote_copy(
            src_ref=wide.at[part, source],
            dst_ref=wide.at[part, source],
            send_sem=fwd_sems.at[0, step - 1, source],
            recv_sem=fwd_sems.at[1, step - 1, source],
            device_id=(dp, core(step)),
            device_id_type=MESH,
        )

    def pair_copy(target):
        return pltpu.make_async_remote_copy(
            src_ref=xout.at[target],
            dst_ref=xin.at[target],
            send_sem=pair_sems.at[0, target],
            recv_sem=pair_sems.at[1, target],
            device_id=(mate, mp),
            device_id_type=MESH,
        )

    def gram_copy(target, source):
        return pltpu.make_async_remote_copy(
            src_ref=gout.at[target],
            dst_ref=gin.at[source],
            send_sem=gram_sems.at[0, target],
            recv_sem=gram_sems.at[1, source],
            device_id=(target * 2 + side, mp),
            device_id_type=MESH,
        )

    def score_copy(step, part):
        return pltpu.make_async_remote_copy(
            src_ref=parts.at[part],
            dst_ref=parts.at[part],
            send_sem=score_sems.at[0, step - 1],
            recv_sem=score_sems.at[1, step - 1],
            device_id=(dp, core(step)),
            device_id_type=MESH,
        )

    barrier = pltpu.get_barrier_semaphore()

    @pl.loop(1, n_dp)
    def _(i):
        pl.semaphore_signal(
            barrier, inc=1, device_id=(lax.rem(dp + i, n_dp), mp), device_id_type=MESH
        )

    for step in range(1, n_mp):
        pl.semaphore_signal(barrier, inc=1, device_id=(dp, core(step)), device_id_type=MESH)
    pl.semaphore_wait(barrier, n_dp - 1 + n_mp - 1)

    @pl.loop(0, R)
    def _(rank):
        rank_copy(rank, side).start()
        held[mp, rank, side] = train_ref[rank]

    @pl.loop(0, split_ranks)
    def _(i):
        placed = None
        for split in range(n_splits):
            term = jnp.dot(
                placing_ref[split],
                query_ref[split * split_ranks + i],
                preferred_element_type=jnp.float32,
            )
            placed = term if placed is None else placed + term
        part = pl.ds(pl.multiple_of(i * width, width), width)
        qout[:, :, part] = placed.astype(qout.dtype).reshape(n_dp, ROWS, width)

    @pl.loop(1, n_dp)
    def _(i):
        query_copy(lax.rem(dp + i, n_dp), dp).start()

    routed_ref[dp] = qout[dp]

    seed = seed_ref[0]
    upper = lax.shift_right_logical(seed, jnp.int32(K.bit_length() - 1))
    spread = as_word(K * hash_factor)
    place = side * n_mp + mp
    inner = lax.broadcasted_iota(jnp.int32, (BLOCK, tile_cols), 0)
    outer = lax.broadcasted_iota(jnp.int32, (BLOCK, tile_cols), 1)

    @pl.loop(0, n_tiles)
    def _(tile):
        column = (place * n_tiles + tile) * tile_cols + outer
        table[tile] = (inner ^ (upper & (BLOCK - 1))) * spread + (
            column ^ (seed & (K - 1))
        ) * hash_factor
        acc[tile] = jnp.zeros(acc.shape[1:], jnp.float32)

    def signs(rank, part, tile):
        pieces = []
        for start in range(0, width, BLOCK):
            base = rank * VW + part * width + start
            mixing = table[tile] + (base ^ (upper & ~(BLOCK - 1))) * spread
            mixing = mixing ^ lax.shift_right_logical(mixing, jnp.full_like(mixing, 16))
            mixing = mixing * last_factor
            pieces.append(
                jnp.where(mixing < 0, jnp.float32(-1), jnp.float32(1)).astype(jnp.bfloat16)
            )
        return jnp.concatenate(pieces, axis=0)

    def project(rank, tile):
        total = None
        for part in range(n_mp):
            term = jnp.dot(
                held[part, rank].reshape(pair_rows, width),
                signs(rank, part, tile),
                preferred_element_type=jnp.float32,
            )
            total = term if total is None else total + term
        acc[tile] += total

    def forward(rank):
        rank_copy(rank, 1 - side).wait_recv()
        for step in range(1, n_mp):
            core_copy(step, mp, rank).start()

    def arrived(rank):
        for step in range(1, n_mp):
            core_copy(step, core(n_mp - step), rank).wait_recv()

    for rank in range(AHEAD):
        forward(rank)

    @pl.loop(0, early)
    def _(rank):
        forward(rank + AHEAD)
        arrived(rank)

        @pl.loop(0, n_tiles)
        def _(tile):
            project(rank, tile)

    @pl.loop(early + AHEAD, R)
    def _(rank):
        forward(rank)

    @pl.loop(early, R)
    def _(rank):
        arrived(rank)

    @pl.loop(0, n_tiles)
    def _(i):
        tile = lax.rem(lax.div(pair, per_tile) + 1 + i, n_tiles)

        @pl.loop(early, R)
        def _(rank):
            project(rank, tile)

        made = (acc[tile] * (1.0 / math.sqrt(L * R * VW))).astype(blocks_ref.dtype)
        for j in range(per_tile):
            target = tile * per_tile + j
            blocks_ref[target] = made[:, j * cols : (j + 1) * cols]

            @pl.when(target != pair)
            def _():
                feat_copy(target, pair).start()

    wide[mp, pair] = blocks_ref[pair]
    for step in range(1, n_mp):
        fwd_copy(step, mp, pair).start()

    @pl.loop(0, others)
    def _(i):
        source = lax.rem(pair + others - i, n_pairs)
        feat_copy(source, source).wait_recv()
        for step in range(1, n_mp):
            fwd_copy(step, mp, source).start()

    @pl.loop(0, n_pairs)
    def _(source):
        for step in range(1, n_mp):
            fwd_copy(step, core(n_mp - step), source).wait_recv()

    row_pairs = n_pairs // n_mp
    row_part = pl.ds(mp * row_pairs, row_pairs)

    @pl.loop(0, n_pairs)
    def _(i):
        target = later(i)
        total = None
        for part in range(n_mp):
            term = lax.dot_general(
                wide[part, target],
                wide[part, row_part].reshape(n_rows, -1),
                (((1,), (1,)), ((), ())),
                preferred_element_type=jnp.float32,
            )
            total = term if total is None else total + term
        keep[target] = total.reshape(2, examples, n_rows)
        xout[target] = keep[target, 1 - side].astype(xout.dtype)
        pair_copy(target).start()

    @pl.loop(0, others)
    def _(i):
        target = later(i)
        pair_copy(target).wait_recv()
        gout[target] = (keep[target, side] + xin[target].astype(jnp.float32)).astype(gout.dtype)
        gram_copy(target, pair).start()

    @pl.loop(1, n_dp)
    def _(i):
        source = lax.rem(dp + n_dp - i, n_dp)
        query_copy(source, source).wait_recv()

    parts[mp] = jnp.zeros(parts.shape[1:], jnp.float32)

    @pl.loop(0, split_ranks)
    def _(i):
        part = pl.ds(pl.multiple_of(i * width, width), width)
        rows = routed_ref[:, :, part].reshape(n_dp * ROWS, width)
        for split in range(n_splits):
            parts[mp] += select_ref[split] * lax.dot_general(
                rows,
                train_ref[split * split_ranks + i],
                (((1,), (1,)), ((), ())),
                preferred_element_type=jnp.float32,
            )

    for step in range(1, n_mp):
        score_copy(step, mp).start()

    pair_copy(pair).wait_recv()
    gram_ref[...] = keep[pair, side] + xin[pair].astype(jnp.float32)

    for step in range(1, n_mp):
        score_copy(step, core(n_mp - step)).wait_recv()
    summed = parts[0]
    for part in range(1, n_mp):
        summed = summed + parts[part]
    scores_ref[...] = summed * (1.0 / (L * math.sqrt(R * VW)))

    @pl.loop(0, others)
    def _(i):
        source = lax.rem(pair + others - i, n_pairs)
        gram_copy(source, source).wait_recv()
        gram_ref[...] += gin[source].astype(jnp.float32)

    gram_ref[...] = gram_ref[...] * (1.0 / math.sqrt(K))

    @pl.loop(0, others)
    def _(i):
        feat_copy(later(i), pair).wait_send()
        gram_copy(later(i), pair).wait_send()

    @pl.loop(0, n_pairs)
    def _(source):
        pair_copy(source).wait_send()
        for step in range(1, n_mp):
            fwd_copy(step, mp, source).wait_send()

    for step in range(1, n_mp):
        score_copy(step, mp).wait_send()

    @pl.loop(0, R)
    def _(rank):
        rank_copy(rank, side).wait_send()
        for step in range(1, n_mp):
            core_copy(step, mp, rank).wait_send()

    @pl.loop(1, n_dp)
    def _(i):
        query_copy(lax.rem(dp + i, n_dp), dp).wait_send()


def trak(seed, train, query, placing, select, n_dp, n_mp):
    n_pairs = n_dp // 2
    examples, width = train.shape[1:]
    n_cols = K // (2 * n_mp)
    cols = n_cols // n_pairs
    tile_cols = max(cols, min(256, n_cols))
    n_tiles = n_cols // tile_cols
    n_rows = n_dp * examples // n_mp
    sums = (n_pairs, examples, n_rows)
    blocks = (n_pairs, 2 * examples, cols)
    queries = (n_dp, ROWS, R // placing.shape[0] * width)
    vmem = pl.BlockSpec(memory_space=pltpu.VMEM)
    return pl.pallas_call(
        functools.partial(trak_kernel, n_mp, R * 3 // 4),
        out_shape=(
            jax.ShapeDtypeStruct((examples, n_rows), jnp.float32),
            jax.ShapeDtypeStruct((n_dp * ROWS, examples), jnp.float32),
        ),
        in_specs=[pl.BlockSpec(memory_space=pltpu.SMEM)] + [vmem] * 4,
        out_specs=(vmem, vmem),
        scratch_shapes=[
            pltpu.VMEM((n_mp, R, 2, examples, width), jnp.bfloat16),
            pltpu.VMEM((n_tiles, BLOCK, tile_cols), jnp.int32),
            pltpu.VMEM((n_tiles, 2 * examples, tile_cols), jnp.float32),
            pltpu.VMEM(blocks, jnp.bfloat16),
            pltpu.VMEM(queries, jnp.bfloat16),
            pltpu.VMEM(queries, jnp.bfloat16),
            pltpu.VMEM((n_mp,) + blocks, jnp.bfloat16),
            pltpu.VMEM((n_pairs, 2, examples, n_rows), jnp.float32),
            pltpu.VMEM(sums, jnp.bfloat16),
            pltpu.VMEM(sums, jnp.bfloat16),
            pltpu.VMEM(sums, jnp.bfloat16),
            pltpu.VMEM(sums, jnp.bfloat16),
            pltpu.VMEM((n_mp, n_dp * ROWS, examples), jnp.float32),
            pltpu.SemaphoreType.DMA((2, R)),
            pltpu.SemaphoreType.DMA((2, n_mp - 1, R)),
            pltpu.SemaphoreType.DMA((2, n_dp)),
            pltpu.SemaphoreType.DMA((2, n_pairs)),
            pltpu.SemaphoreType.DMA((2, n_mp - 1, n_pairs)),
            pltpu.SemaphoreType.DMA((2, n_pairs)),
            pltpu.SemaphoreType.DMA((2, n_pairs)),
            pltpu.SemaphoreType.DMA((2, n_mp - 1)),
        ],
        compiler_params=pltpu.CompilerParams(
            collective_id=0, has_side_effects=True, vmem_limit_bytes=48 * 2**20
        ),
        name="trak",
    )(seed, train, query, placing, select)


def shards(train_in, train_out_grad, query_in, query_out_grad, query_owner, sketch_seed):
    n_mp = lax.axis_size("mp")
    n_dp = lax.axis_size("dp")
    train_grads = local_grads(train_in, train_out_grad)
    query_grads = local_grads(query_in, query_out_grad)
    _, queries, _ = query_grads.shape
    examples = train_grads.shape[1]
    capacity = 2 * queries // n_dp
    n_splits = ROWS // capacity

    with jax.named_scope("placing"):
        owners = query_owner[:, 0]
        later_index = lax.broadcasted_iota(jnp.int32, (queries, queries), 0)
        earlier = (owners[:, None] == owners[None, :]) & (
            lax.broadcasted_iota(jnp.int32, (queries, queries), 1) < later_index
        )
        slot_rank = jnp.sum(earlier.astype(jnp.int32), axis=1)
        target = owners * ROWS + slot_rank
        shape = (n_splits, n_dp * ROWS, queries)
        split_ids = lax.broadcasted_iota(jnp.int32, shape, 0)
        row_ids = lax.broadcasted_iota(jnp.int32, shape, 1)
        placing = (row_ids == target[None, None, :] + split_ids * capacity).astype(jnp.bfloat16)
        shape = (n_splits, n_dp * ROWS, examples)
        split_ids = lax.broadcasted_iota(jnp.int32, shape, 0)
        row_ids = lax.broadcasted_iota(jnp.int32, shape, 1)
        select = (row_ids % ROWS // capacity == split_ids).astype(jnp.float32)

    gram, scores = trak(sketch_seed, train_grads, query_grads, placing, select, n_dp, n_mp)
    scores = jnp.sum(scores.reshape(n_dp, n_splits, capacity, examples), axis=1)
    return (gram.T, scores[None])


def solution(mesh):
    return jax.shard_map(
        shards,
        mesh=mesh,
        in_specs=(
            P("dp", None, None),
            P("dp", None, "mp"),
            P("dp", None, None),
            P("dp", None, "mp"),
            P("dp", None),
            P(),
        ),
        out_specs=(P("mp", "dp"), P("dp", None, None, None)),
        check_vma=False,
    )
```

```python
import functools
import math

import jax
import jax.numpy as jnp
from jax import lax
from jax.experimental import pallas as pl
from jax.experimental.pallas import tpu as pltpu
from jax.sharding import PartitionSpec as P

VW = 1024
R = 16
K = 8192
L = 64
BLOCK = 64
ROWS = 16
AHEAD = 2

hash_factor = 73244475


def as_word(value):
    value &= 0xFFFFFFFF
    return value - (1 << 32) if value >= 1 << 31 else value


last_factor = as_word((hash_factor + 65536) << 15)


def local_grads(inputs, out_grads):
    return jnp.einsum("ntr,ntj->rnj", inputs, out_grads, preferred_element_type=jnp.float32).astype(
        jnp.bfloat16
    )


MESH = pl.DeviceIdType.MESH


def trak_kernel(
    n_mp,
    early,
    seed_ref,
    train_ref,
    query_ref,
    placing_ref,
    select_ref,
    gram_ref,
    scores_ref,
    held,
    table,
    acc,
    blocks_ref,
    qout,
    routed_ref,
    wide,
    keep,
    xout,
    xin,
    gout,
    gin,
    parts,
    rank_sems,
    core_sems,
    query_sems,
    feat_sems,
    fwd_sems,
    pair_sems,
    gram_sems,
    score_sems,
):
    n_pairs, pair_rows, cols = blocks_ref.shape
    n_dp = routed_ref.shape[0]
    n_tiles, _, tile_cols = table.shape
    per_tile = tile_cols // cols
    width = train_ref.shape[2]
    n_splits = placing_ref.shape[0]
    split_ranks = R // n_splits
    examples = pair_rows // 2
    n_rows = n_pairs * pair_rows // n_mp
    dp = lax.axis_index("dp")
    mp = lax.axis_index("mp")
    pair = dp // 2
    side = dp % 2
    mate = pair * 2 + 1 - side
    others = n_pairs - 1

    def later(i):
        return lax.rem(pair + 1 + i, n_pairs)

    def core(step):
        return lax.rem(mp + step, n_mp)

    def rank_copy(rank, rows):
        return pltpu.make_async_remote_copy(
            src_ref=train_ref.at[rank],
            dst_ref=held.at[mp, rank, rows],
            send_sem=rank_sems.at[0, rank],
            recv_sem=rank_sems.at[1, rank],
            device_id=(mate, mp),
            device_id_type=MESH,
        )

    def core_copy(step, part, rank):
        return pltpu.make_async_remote_copy(
            src_ref=held.at[part, rank],
            dst_ref=held.at[part, rank],
            send_sem=core_sems.at[0, step - 1, rank],
            recv_sem=core_sems.at[1, step - 1, rank],
            device_id=(dp, core(step)),
            device_id_type=MESH,
        )

    def query_copy(target, source):
        return pltpu.make_async_remote_copy(
            src_ref=qout.at[target],
            dst_ref=routed_ref.at[source],
            send_sem=query_sems.at[0, target],
            recv_sem=query_sems.at[1, source],
            device_id=(target, mp),
            device_id_type=MESH,
        )

    def feat_copy(target, source):
        return pltpu.make_async_remote_copy(
            src_ref=blocks_ref.at[target],
            dst_ref=wide.at[mp, source],
            send_sem=feat_sems.at[0, target],
            recv_sem=feat_sems.at[1, source],
            device_id=(target * 2 + side, mp),
            device_id_type=MESH,
        )

    def fwd_copy(step, part, source):
        return pltpu.make_async_remote_copy(
            src_ref=wide.at[part, source],
            dst_ref=wide.at[part, source],
            send_sem=fwd_sems.at[0, step - 1, source],
            recv_sem=fwd_sems.at[1, step - 1, source],
            device_id=(dp, core(step)),
            device_id_type=MESH,
        )

    def pair_copy(target):
        return pltpu.make_async_remote_copy(
            src_ref=xout.at[target],
            dst_ref=xin.at[target],
            send_sem=pair_sems.at[0, target],
            recv_sem=pair_sems.at[1, target],
            device_id=(mate, mp),
            device_id_type=MESH,
        )

    def gram_copy(target, source):
        return pltpu.make_async_remote_copy(
            src_ref=gout.at[target],
            dst_ref=gin.at[source],
            send_sem=gram_sems.at[0, target],
            recv_sem=gram_sems.at[1, source],
            device_id=(target * 2 + side, mp),
            device_id_type=MESH,
        )

    def score_copy(step, part):
        return pltpu.make_async_remote_copy(
            src_ref=parts.at[part],
            dst_ref=parts.at[part],
            send_sem=score_sems.at[0, step - 1],
            recv_sem=score_sems.at[1, step - 1],
            device_id=(dp, core(step)),
            device_id_type=MESH,
        )

    barrier = pltpu.get_barrier_semaphore()

    @pl.loop(1, n_dp)
    def _(i):
        pl.semaphore_signal(
            barrier, inc=1, device_id=(lax.rem(dp + i, n_dp), mp), device_id_type=MESH
        )

    for step in range(1, n_mp):
        pl.semaphore_signal(barrier, inc=1, device_id=(dp, core(step)), device_id_type=MESH)
    pl.semaphore_wait(barrier, n_dp - 1 + n_mp - 1)

    @pl.loop(0, R)
    def _(rank):
        rank_copy(rank, side).start()
        held[mp, rank, side] = train_ref[rank]

    @pl.loop(0, split_ranks)
    def _(i):
        placed = None
        for split in range(n_splits):
            term = jnp.dot(
                placing_ref[split],
                query_ref[split * split_ranks + i],
                preferred_element_type=jnp.float32,
            )
            placed = term if placed is None else placed + term
        part = pl.ds(pl.multiple_of(i * width, width), width)
        qout[:, :, part] = placed.astype(qout.dtype).reshape(n_dp, ROWS, width)

    stride = next(i for i in (5, 3, 7, 1) if math.gcd(i, n_dp) == 1)

    routed_ref[dp] = qout[dp]

    seed = seed_ref[0]
    upper = lax.shift_right_logical(seed, jnp.int32(K.bit_length() - 1))
    spread = as_word(K * hash_factor)
    place = side * n_mp + mp
    inner = lax.broadcasted_iota(jnp.int32, (BLOCK, tile_cols), 0)
    outer = lax.broadcasted_iota(jnp.int32, (BLOCK, tile_cols), 1)

    @pl.loop(0, n_tiles)
    def _(tile):
        column = (place * n_tiles + tile) * tile_cols + outer
        table[tile] = (inner ^ (upper & (BLOCK - 1))) * spread + (
            column ^ (seed & (K - 1))
        ) * hash_factor
        acc[tile] = jnp.zeros(acc.shape[1:], jnp.float32)

    def signs(rank, part, tile):
        pieces = []
        for start in range(0, width, BLOCK):
            base = rank * VW + part * width + start
            mixing = table[tile] + (base ^ (upper & ~(BLOCK - 1))) * spread
            mixing = mixing ^ lax.shift_right_logical(mixing, jnp.full_like(mixing, 16))
            mixing = mixing * last_factor
            pieces.append(
                jnp.where(mixing < 0, jnp.float32(-1), jnp.float32(1)).astype(jnp.bfloat16)
            )
        return jnp.concatenate(pieces, axis=0)

    def project(rank, tile):
        total = None
        for part in range(n_mp):
            term = jnp.dot(
                held[part, rank].reshape(pair_rows, width),
                signs(rank, part, tile),
                preferred_element_type=jnp.float32,
            )
            total = term if total is None else total + term
        acc[tile] += total

    def forward(rank):
        rank_copy(rank, 1 - side).wait_recv()
        for step in range(1, n_mp):
            core_copy(step, mp, rank).start()

    def arrived(rank):
        for step in range(1, n_mp):
            core_copy(step, core(n_mp - step), rank).wait_recv()

    for rank in range(AHEAD):
        forward(rank)

    @pl.loop(0, early)
    def _(rank):
        forward(rank + AHEAD)
        arrived(rank)

        @pl.loop(1 + rank * (n_dp - 1) // early, 1 + (rank + 1) * (n_dp - 1) // early)
        def _(i):
            query_copy(lax.rem(dp + i * stride, n_dp), dp).start()

        @pl.loop(0, n_tiles)
        def _(tile):
            project(rank, tile)

    @pl.loop(early + AHEAD, R)
    def _(rank):
        forward(rank)

    @pl.loop(early, R)
    def _(rank):
        arrived(rank)

    @pl.loop(0, n_tiles)
    def _(i):
        tile = lax.rem(lax.div(pair, per_tile) + 1 + i, n_tiles)

        @pl.loop(early, R)
        def _(rank):
            project(rank, tile)

        made = (acc[tile] * (1.0 / math.sqrt(L * R * VW))).astype(blocks_ref.dtype)
        for j in range(per_tile):
            target = tile * per_tile + j
            blocks_ref[target] = made[:, j * cols : (j + 1) * cols]

            @pl.when(target != pair)
            def _():
                feat_copy(target, pair).start()

    wide[mp, pair] = blocks_ref[pair]
    for step in range(1, n_mp):
        fwd_copy(step, mp, pair).start()

    @pl.loop(0, others)
    def _(i):
        source = lax.rem(pair + others - i, n_pairs)
        feat_copy(source, source).wait_recv()
        for step in range(1, n_mp):
            fwd_copy(step, mp, source).start()

    @pl.loop(0, n_pairs)
    def _(source):
        for step in range(1, n_mp):
            fwd_copy(step, core(n_mp - step), source).wait_recv()

    row_pairs = n_pairs // n_mp
    row_part = pl.ds(mp * row_pairs, row_pairs)

    @pl.loop(0, n_pairs)
    def _(i):
        target = later(i)
        total = None
        for part in range(n_mp):
            term = lax.dot_general(
                wide[part, target],
                wide[part, row_part].reshape(n_rows, -1),
                (((1,), (1,)), ((), ())),
                preferred_element_type=jnp.float32,
            )
            total = term if total is None else total + term
        keep[target] = total.reshape(2, examples, n_rows)
        xout[target] = keep[target, 1 - side].astype(xout.dtype)
        pair_copy(target).start()

    @pl.loop(0, others)
    def _(i):
        target = later(i)
        pair_copy(target).wait_recv()
        gout[target] = (keep[target, side] + xin[target].astype(jnp.float32)).astype(gout.dtype)
        gram_copy(target, pair).start()

    @pl.loop(1, n_dp)
    def _(i):
        source = lax.rem(dp + n_dp - i, n_dp)
        query_copy(source, source).wait_recv()

    parts[mp] = jnp.zeros(parts.shape[1:], jnp.float32)

    @pl.loop(0, split_ranks)
    def _(i):
        part = pl.ds(pl.multiple_of(i * width, width), width)
        rows = routed_ref[:, :, part].reshape(n_dp * ROWS, width)
        for split in range(n_splits):
            parts[mp] += select_ref[split] * lax.dot_general(
                rows,
                train_ref[split * split_ranks + i],
                (((1,), (1,)), ((), ())),
                preferred_element_type=jnp.float32,
            )

    for step in range(1, n_mp):
        score_copy(step, mp).start()

    pair_copy(pair).wait_recv()
    gram_ref[...] = keep[pair, side] + xin[pair].astype(jnp.float32)

    for step in range(1, n_mp):
        score_copy(step, core(n_mp - step)).wait_recv()
    summed = parts[0]
    for part in range(1, n_mp):
        summed = summed + parts[part]
    scores_ref[...] = summed * (1.0 / (L * math.sqrt(R * VW)))

    @pl.loop(0, others)
    def _(i):
        source = lax.rem(pair + others - i, n_pairs)
        gram_copy(source, source).wait_recv()
        gram_ref[...] += gin[source].astype(jnp.float32)

    gram_ref[...] = gram_ref[...] * (1.0 / math.sqrt(K))

    @pl.loop(0, others)
    def _(i):
        feat_copy(later(i), pair).wait_send()
        gram_copy(later(i), pair).wait_send()

    @pl.loop(0, n_pairs)
    def _(source):
        pair_copy(source).wait_send()
        for step in range(1, n_mp):
            fwd_copy(step, mp, source).wait_send()

    for step in range(1, n_mp):
        score_copy(step, mp).wait_send()

    @pl.loop(0, R)
    def _(rank):
        rank_copy(rank, side).wait_send()
        for step in range(1, n_mp):
            core_copy(step, mp, rank).wait_send()

    @pl.loop(1, n_dp)
    def _(i):
        query_copy(lax.rem(dp + i, n_dp), dp).wait_send()


def trak(seed, train, query, placing, select, n_dp, n_mp):
    n_pairs = n_dp // 2
    examples, width = train.shape[1:]
    n_cols = K // (2 * n_mp)
    cols = n_cols // n_pairs
    tile_cols = max(cols, min(256, n_cols))
    n_tiles = n_cols // tile_cols
    n_rows = n_dp * examples // n_mp
    sums = (n_pairs, examples, n_rows)
    blocks = (n_pairs, 2 * examples, cols)
    queries = (n_dp, ROWS, R // placing.shape[0] * width)
    vmem = pl.BlockSpec(memory_space=pltpu.VMEM)
    return pl.pallas_call(
        functools.partial(trak_kernel, n_mp, R * 3 // 4),
        out_shape=(
            jax.ShapeDtypeStruct((examples, n_rows), jnp.float32),
            jax.ShapeDtypeStruct((n_dp * ROWS, examples), jnp.float32),
        ),
        in_specs=[pl.BlockSpec(memory_space=pltpu.SMEM)] + [vmem] * 4,
        out_specs=(vmem, vmem),
        scratch_shapes=[
            pltpu.VMEM((n_mp, R, 2, examples, width), jnp.bfloat16),
            pltpu.VMEM((n_tiles, BLOCK, tile_cols), jnp.int32),
            pltpu.VMEM((n_tiles, 2 * examples, tile_cols), jnp.float32),
            pltpu.VMEM(blocks, jnp.bfloat16),
            pltpu.VMEM(queries, jnp.bfloat16),
            pltpu.VMEM(queries, jnp.bfloat16),
            pltpu.VMEM((n_mp,) + blocks, jnp.bfloat16),
            pltpu.VMEM((n_pairs, 2, examples, n_rows), jnp.float32),
            pltpu.VMEM(sums, jnp.bfloat16),
            pltpu.VMEM(sums, jnp.bfloat16),
            pltpu.VMEM(sums, jnp.bfloat16),
            pltpu.VMEM(sums, jnp.bfloat16),
            pltpu.VMEM((n_mp, n_dp * ROWS, examples), jnp.float32),
            pltpu.SemaphoreType.DMA((2, R)),
            pltpu.SemaphoreType.DMA((2, n_mp - 1, R)),
            pltpu.SemaphoreType.DMA((2, n_dp)),
            pltpu.SemaphoreType.DMA((2, n_pairs)),
            pltpu.SemaphoreType.DMA((2, n_mp - 1, n_pairs)),
            pltpu.SemaphoreType.DMA((2, n_pairs)),
            pltpu.SemaphoreType.DMA((2, n_pairs)),
            pltpu.SemaphoreType.DMA((2, n_mp - 1)),
        ],
        compiler_params=pltpu.CompilerParams(
            collective_id=0, has_side_effects=True, vmem_limit_bytes=48 * 2**20
        ),
        name="trak",
    )(seed, train, query, placing, select)


def shards(train_in, train_out_grad, query_in, query_out_grad, query_owner, sketch_seed):
    n_mp = lax.axis_size("mp")
    n_dp = lax.axis_size("dp")
    train_grads = local_grads(train_in, train_out_grad)
    query_grads = local_grads(query_in, query_out_grad)
    _, queries, _ = query_grads.shape
    examples = train_grads.shape[1]
    capacity = 2 * queries // n_dp
    n_splits = ROWS // capacity

    with jax.named_scope("placing"):
        owners = query_owner[:, 0]
        later_index = lax.broadcasted_iota(jnp.int32, (queries, queries), 0)
        earlier = (owners[:, None] == owners[None, :]) & (
            lax.broadcasted_iota(jnp.int32, (queries, queries), 1) < later_index
        )
        slot_rank = jnp.sum(earlier.astype(jnp.int32), axis=1)
        target = owners * ROWS + slot_rank
        shape = (n_splits, n_dp * ROWS, queries)
        split_ids = lax.broadcasted_iota(jnp.int32, shape, 0)
        row_ids = lax.broadcasted_iota(jnp.int32, shape, 1)
        placing = (row_ids == target[None, None, :] + split_ids * capacity).astype(jnp.bfloat16)
        shape = (n_splits, n_dp * ROWS, examples)
        split_ids = lax.broadcasted_iota(jnp.int32, shape, 0)
        row_ids = lax.broadcasted_iota(jnp.int32, shape, 1)
        select = (row_ids % ROWS // capacity == split_ids).astype(jnp.float32)

    gram, scores = trak(sketch_seed, train_grads, query_grads, placing, select, n_dp, n_mp)
    scores = jnp.sum(scores.reshape(n_dp, n_splits, capacity, examples), axis=1)
    return (gram.T, scores[None])


def solution(mesh):
    return jax.shard_map(
        shards,
        mesh=mesh,
        in_specs=(
            P("dp", None, None),
            P("dp", None, "mp"),
            P("dp", None, None),
            P("dp", None, "mp"),
            P("dp", None),
            P(),
        ),
        out_specs=(P("mp", "dp"), P("dp", None, None, None)),
        check_vma=False,
    )
```

```python
import functools
import math

import jax
import jax.numpy as jnp
from jax import lax
from jax.experimental import pallas as pl
from jax.experimental.pallas import tpu as pltpu
from jax.sharding import PartitionSpec as P

VW = 1024
R = 16
K = 8192
L = 64
BLOCK = 32
ROWS = 16
AHEAD = 2

hash_factor = 73244475


def as_word(value):
    value &= 0xFFFFFFFF
    return value - (1 << 32) if value >= 1 << 31 else value


last_factor = as_word((hash_factor + 65536) << 15)


def local_grads(inputs, out_grads):
    return jnp.einsum("ntr,ntj->rnj", inputs, out_grads, preferred_element_type=jnp.float32).astype(
        jnp.bfloat16
    )


MESH = pl.DeviceIdType.MESH


def trak_kernel(
    n_mp,
    early,
    seed_ref,
    train_ref,
    query_ref,
    placing_ref,
    select_ref,
    gram_ref,
    scores_ref,
    held,
    table,
    acc,
    blocks_ref,
    qout,
    routed_ref,
    wide,
    keep,
    xout,
    xin,
    gout,
    gin,
    parts,
    rank_sems,
    core_sems,
    query_sems,
    feat_sems,
    fwd_sems,
    pair_sems,
    gram_sems,
    score_sems,
):
    n_pairs, pair_rows, cols = blocks_ref.shape
    n_dp = routed_ref.shape[0]
    n_tiles, _, tile_cols = table.shape
    per_tile = tile_cols // cols
    width = train_ref.shape[2]
    n_splits = placing_ref.shape[0]
    split_ranks = R // n_splits
    examples = pair_rows // 2
    n_rows = n_pairs * pair_rows // n_mp
    dp = lax.axis_index("dp")
    mp = lax.axis_index("mp")
    pair = dp // 2
    side = dp % 2
    mate = pair * 2 + 1 - side
    others = n_pairs - 1

    def later(i):
        return lax.rem(pair + 1 + i, n_pairs)

    def core(step):
        return lax.rem(mp + step, n_mp)

    def rank_copy(rank, rows):
        return pltpu.make_async_remote_copy(
            src_ref=train_ref.at[rank],
            dst_ref=held.at[mp, rank, rows],
            send_sem=rank_sems.at[0, rank],
            recv_sem=rank_sems.at[1, rank],
            device_id=(mate, mp),
            device_id_type=MESH,
        )

    def core_copy(step, part, rank):
        return pltpu.make_async_remote_copy(
            src_ref=held.at[part, rank],
            dst_ref=held.at[part, rank],
            send_sem=core_sems.at[0, step - 1, rank],
            recv_sem=core_sems.at[1, step - 1, rank],
            device_id=(dp, core(step)),
            device_id_type=MESH,
        )

    def query_copy(target, source):
        return pltpu.make_async_remote_copy(
            src_ref=qout.at[target],
            dst_ref=routed_ref.at[source],
            send_sem=query_sems.at[0, target],
            recv_sem=query_sems.at[1, source],
            device_id=(target, mp),
            device_id_type=MESH,
        )

    def feat_copy(target, source):
        return pltpu.make_async_remote_copy(
            src_ref=blocks_ref.at[target],
            dst_ref=wide.at[mp, source],
            send_sem=feat_sems.at[0, target],
            recv_sem=feat_sems.at[1, source],
            device_id=(target * 2 + side, mp),
            device_id_type=MESH,
        )

    def fwd_copy(step, part, source):
        return pltpu.make_async_remote_copy(
            src_ref=wide.at[part, source],
            dst_ref=wide.at[part, source],
            send_sem=fwd_sems.at[0, step - 1, source],
            recv_sem=fwd_sems.at[1, step - 1, source],
            device_id=(dp, core(step)),
            device_id_type=MESH,
        )

    def pair_copy(target):
        return pltpu.make_async_remote_copy(
            src_ref=xout.at[target],
            dst_ref=xin.at[target],
            send_sem=pair_sems.at[0, target],
            recv_sem=pair_sems.at[1, target],
            device_id=(mate, mp),
            device_id_type=MESH,
        )

    def gram_copy(target, source):
        return pltpu.make_async_remote_copy(
            src_ref=gout.at[target],
            dst_ref=gin.at[source],
            send_sem=gram_sems.at[0, target],
            recv_sem=gram_sems.at[1, source],
            device_id=(target * 2 + side, mp),
            device_id_type=MESH,
        )

    def score_copy(step, part):
        return pltpu.make_async_remote_copy(
            src_ref=parts.at[part],
            dst_ref=parts.at[part],
            send_sem=score_sems.at[0, step - 1],
            recv_sem=score_sems.at[1, step - 1],
            device_id=(dp, core(step)),
            device_id_type=MESH,
        )

    barrier = pltpu.get_barrier_semaphore()

    @pl.loop(1, n_dp)
    def _(i):
        pl.semaphore_signal(
            barrier, inc=1, device_id=(lax.rem(dp + i, n_dp), mp), device_id_type=MESH
        )

    for step in range(1, n_mp):
        pl.semaphore_signal(barrier, inc=1, device_id=(dp, core(step)), device_id_type=MESH)
    pl.semaphore_wait(barrier, n_dp - 1 + n_mp - 1)

    @pl.loop(0, R)
    def _(rank):
        rank_copy(rank, side).start()
        held[mp, rank, side] = train_ref[rank]

    @pl.loop(0, split_ranks)
    def _(i):
        placed = None
        for split in range(n_splits):
            term = jnp.dot(
                placing_ref[split],
                query_ref[split * split_ranks + i],
                preferred_element_type=jnp.float32,
            )
            placed = term if placed is None else placed + term
        part = pl.ds(pl.multiple_of(i * width, width), width)
        qout[:, :, part] = placed.astype(qout.dtype).reshape(n_dp, ROWS, width)

    @pl.loop(1, n_dp)
    def _(i):
        query_copy(lax.rem(dp + i, n_dp), dp).start()

    routed_ref[dp] = qout[dp]

    seed = seed_ref[0]
    upper = lax.shift_right_logical(seed, jnp.int32(K.bit_length() - 1))
    spread = as_word(K * hash_factor)
    place = side * n_mp + mp
    inner = lax.broadcasted_iota(jnp.int32, (BLOCK, tile_cols), 0)
    outer = lax.broadcasted_iota(jnp.int32, (BLOCK, tile_cols), 1)

    @pl.loop(0, n_tiles)
    def _(tile):
        column = (place * n_tiles + tile) * tile_cols + outer
        table[tile] = (inner ^ (upper & (BLOCK - 1))) * spread + (
            column ^ (seed & (K - 1))
        ) * hash_factor
        acc[tile] = jnp.zeros(acc.shape[1:], jnp.float32)

    def signs(rank, part, tile):
        pieces = []
        for start in range(0, width, BLOCK):
            base = rank * VW + part * width + start
            mixing = table[tile] + (base ^ (upper & ~(BLOCK - 1))) * spread
            mixing = mixing ^ lax.shift_right_logical(mixing, jnp.full_like(mixing, 16))
            mixing = mixing * last_factor
            pieces.append(
                jnp.where(mixing < 0, jnp.float32(-1), jnp.float32(1)).astype(jnp.bfloat16)
            )
        return jnp.concatenate(pieces, axis=0)

    def project(rank, tile):
        total = None
        for part in range(n_mp):
            term = jnp.dot(
                held[part, rank].reshape(pair_rows, width),
                signs(rank, part, tile),
                preferred_element_type=jnp.float32,
            )
            total = term if total is None else total + term
        acc[tile] += total

    def forward(rank):
        rank_copy(rank, 1 - side).wait_recv()
        for step in range(1, n_mp):
            core_copy(step, mp, rank).start()

    def arrived(rank):
        for step in range(1, n_mp):
            core_copy(step, core(n_mp - step), rank).wait_recv()

    for rank in range(AHEAD):
        forward(rank)

    @pl.loop(0, early)
    def _(rank):
        forward(rank + AHEAD)
        arrived(rank)

        @pl.loop(0, n_tiles)
        def _(tile):
            project(rank, tile)

    @pl.loop(early + AHEAD, R)
    def _(rank):
        forward(rank)

    @pl.loop(early, R)
    def _(rank):
        arrived(rank)

    @pl.loop(0, n_tiles)
    def _(i):
        tile = lax.rem(lax.div(pair, per_tile) + 1 + i, n_tiles)

        @pl.loop(early, R)
        def _(rank):
            project(rank, tile)

        made = (acc[tile] * (1.0 / math.sqrt(L * R * VW))).astype(blocks_ref.dtype)
        for j in range(per_tile):
            target = tile * per_tile + j
            blocks_ref[target] = made[:, j * cols : (j + 1) * cols]

            @pl.when(target != pair)
            def _():
                feat_copy(target, pair).start()

    wide[mp, pair] = blocks_ref[pair]
    for step in range(1, n_mp):
        fwd_copy(step, mp, pair).start()

    @pl.loop(0, others)
    def _(i):
        source = lax.rem(pair + others - i, n_pairs)
        feat_copy(source, source).wait_recv()
        for step in range(1, n_mp):
            fwd_copy(step, mp, source).start()

    @pl.loop(0, n_pairs)
    def _(source):
        for step in range(1, n_mp):
            fwd_copy(step, core(n_mp - step), source).wait_recv()

    row_pairs = n_pairs // n_mp
    row_part = pl.ds(mp * row_pairs, row_pairs)

    @pl.loop(0, n_pairs)
    def _(i):
        target = later(i)
        total = None
        for part in range(n_mp):
            term = lax.dot_general(
                wide[part, target],
                wide[part, row_part].reshape(n_rows, -1),
                (((1,), (1,)), ((), ())),
                preferred_element_type=jnp.float32,
            )
            total = term if total is None else total + term
        keep[target] = total.reshape(2, examples, n_rows)
        xout[target] = keep[target, 1 - side].astype(xout.dtype)
        pair_copy(target).start()

    @pl.loop(0, others)
    def _(i):
        target = later(i)
        pair_copy(target).wait_recv()
        gout[target] = (keep[target, side] + xin[target].astype(jnp.float32)).astype(gout.dtype)
        gram_copy(target, pair).start()

    @pl.loop(1, n_dp)
    def _(i):
        source = lax.rem(dp + n_dp - i, n_dp)
        query_copy(source, source).wait_recv()

    parts[mp] = jnp.zeros(parts.shape[1:], jnp.float32)

    @pl.loop(0, split_ranks)
    def _(i):
        part = pl.ds(pl.multiple_of(i * width, width), width)
        rows = routed_ref[:, :, part].reshape(n_dp * ROWS, width)
        for split in range(n_splits):
            parts[mp] += select_ref[split] * lax.dot_general(
                rows,
                train_ref[split * split_ranks + i],
                (((1,), (1,)), ((), ())),
                preferred_element_type=jnp.float32,
            )

    for step in range(1, n_mp):
        score_copy(step, mp).start()

    pair_copy(pair).wait_recv()
    gram_ref[...] = keep[pair, side] + xin[pair].astype(jnp.float32)

    for step in range(1, n_mp):
        score_copy(step, core(n_mp - step)).wait_recv()
    summed = parts[0]
    for part in range(1, n_mp):
        summed = summed + parts[part]
    scores_ref[...] = summed * (1.0 / (L * math.sqrt(R * VW)))

    @pl.loop(0, others)
    def _(i):
        source = lax.rem(pair + others - i, n_pairs)
        gram_copy(source, source).wait_recv()
        gram_ref[...] += gin[source].astype(jnp.float32)

    gram_ref[...] = gram_ref[...] * (1.0 / math.sqrt(K))

    @pl.loop(0, others)
    def _(i):
        feat_copy(later(i), pair).wait_send()
        gram_copy(later(i), pair).wait_send()

    @pl.loop(0, n_pairs)
    def _(source):
        pair_copy(source).wait_send()
        for step in range(1, n_mp):
            fwd_copy(step, mp, source).wait_send()

    for step in range(1, n_mp):
        score_copy(step, mp).wait_send()

    @pl.loop(0, R)
    def _(rank):
        rank_copy(rank, side).wait_send()
        for step in range(1, n_mp):
            core_copy(step, mp, rank).wait_send()

    @pl.loop(1, n_dp)
    def _(i):
        query_copy(lax.rem(dp + i, n_dp), dp).wait_send()


def trak(seed, train, query, placing, select, n_dp, n_mp):
    n_pairs = n_dp // 2
    examples, width = train.shape[1:]
    n_cols = K // (2 * n_mp)
    cols = n_cols // n_pairs
    tile_cols = max(cols, min(512, n_cols))
    n_tiles = n_cols // tile_cols
    n_rows = n_dp * examples // n_mp
    sums = (n_pairs, examples, n_rows)
    blocks = (n_pairs, 2 * examples, cols)
    queries = (n_dp, ROWS, R // placing.shape[0] * width)
    vmem = pl.BlockSpec(memory_space=pltpu.VMEM)
    return pl.pallas_call(
        functools.partial(trak_kernel, n_mp, R * 3 // 4),
        out_shape=(
            jax.ShapeDtypeStruct((examples, n_rows), jnp.float32),
            jax.ShapeDtypeStruct((n_dp * ROWS, examples), jnp.float32),
        ),
        in_specs=[pl.BlockSpec(memory_space=pltpu.SMEM)] + [vmem] * 4,
        out_specs=(vmem, vmem),
        scratch_shapes=[
            pltpu.VMEM((n_mp, R, 2, examples, width), jnp.bfloat16),
            pltpu.VMEM((n_tiles, BLOCK, tile_cols), jnp.int32),
            pltpu.VMEM((n_tiles, 2 * examples, tile_cols), jnp.float32),
            pltpu.VMEM(blocks, jnp.bfloat16),
            pltpu.VMEM(queries, jnp.bfloat16),
            pltpu.VMEM(queries, jnp.bfloat16),
            pltpu.VMEM((n_mp,) + blocks, jnp.bfloat16),
            pltpu.VMEM((n_pairs, 2, examples, n_rows), jnp.float32),
            pltpu.VMEM(sums, jnp.bfloat16),
            pltpu.VMEM(sums, jnp.bfloat16),
            pltpu.VMEM(sums, jnp.bfloat16),
            pltpu.VMEM(sums, jnp.bfloat16),
            pltpu.VMEM((n_mp, n_dp * ROWS, examples), jnp.float32),
            pltpu.SemaphoreType.DMA((2, R)),
            pltpu.SemaphoreType.DMA((2, n_mp - 1, R)),
            pltpu.SemaphoreType.DMA((2, n_dp)),
            pltpu.SemaphoreType.DMA((2, n_pairs)),
            pltpu.SemaphoreType.DMA((2, n_mp - 1, n_pairs)),
            pltpu.SemaphoreType.DMA((2, n_pairs)),
            pltpu.SemaphoreType.DMA((2, n_pairs)),
            pltpu.SemaphoreType.DMA((2, n_mp - 1)),
        ],
        compiler_params=pltpu.CompilerParams(
            collective_id=0, has_side_effects=True, vmem_limit_bytes=48 * 2**20
        ),
        name="trak",
    )(seed, train, query, placing, select)


def shards(train_in, train_out_grad, query_in, query_out_grad, query_owner, sketch_seed):
    n_mp = lax.axis_size("mp")
    n_dp = lax.axis_size("dp")
    train_grads = local_grads(train_in, train_out_grad)
    query_grads = local_grads(query_in, query_out_grad)
    _, queries, _ = query_grads.shape
    examples = train_grads.shape[1]
    capacity = 2 * queries // n_dp
    n_splits = ROWS // capacity

    with jax.named_scope("placing"):
        owners = query_owner[:, 0]
        later_index = lax.broadcasted_iota(jnp.int32, (queries, queries), 0)
        earlier = (owners[:, None] == owners[None, :]) & (
            lax.broadcasted_iota(jnp.int32, (queries, queries), 1) < later_index
        )
        slot_rank = jnp.sum(earlier.astype(jnp.int32), axis=1)
        target = owners * ROWS + slot_rank
        shape = (n_splits, n_dp * ROWS, queries)
        split_ids = lax.broadcasted_iota(jnp.int32, shape, 0)
        row_ids = lax.broadcasted_iota(jnp.int32, shape, 1)
        placing = (row_ids == target[None, None, :] + split_ids * capacity).astype(jnp.bfloat16)
        shape = (n_splits, n_dp * ROWS, examples)
        split_ids = lax.broadcasted_iota(jnp.int32, shape, 0)
        row_ids = lax.broadcasted_iota(jnp.int32, shape, 1)
        select = (row_ids % ROWS // capacity == split_ids).astype(jnp.float32)

    gram, scores = trak(sketch_seed, train_grads, query_grads, placing, select, n_dp, n_mp)
    scores = jnp.sum(scores.reshape(n_dp, n_splits, capacity, examples), axis=1)
    return (gram.T, scores[None])


def solution(mesh):
    return jax.shard_map(
        shards,
        mesh=mesh,
        in_specs=(
            P("dp", None, None),
            P("dp", None, "mp"),
            P("dp", None, None),
            P("dp", None, "mp"),
            P("dp", None),
            P(),
        ),
        out_specs=(P("mp", "dp"), P("dp", None, None, None)),
        check_vma=False,
    )
```
